512 devices in a mesh: section: 32 (over x_hi, z, core), head: 16 (over y, x_lo).
Axes of the slice: x: 4 (x_hi: 2, x_lo: 2; x = x_hi * 2 + x_lo), y: 8, z: 8, core: 2. Of those that a mesh axis runs over, the one named last changes fastest.
Arguments:
- out_grad: bfloat16 [8192, 8192], P('section', 'head'), may hold values from -6 to 6
- held_query: bfloat16 [8192, 8192], P('section', 'head'), may hold values from -90 to 90
- held_output: bfloat16 [8192, 8192], P('section', 'head'), may hold values from -6 to 6
- key_cache: bfloat16 [40960, 512], P(('section', 'head')), may hold values from -4 to 4
- value_cache: bfloat16 [40960, 512], P(('section', 'head')), may hold values from -6 to 6
- segment_ids: int32 [8192], P('section'), may hold values from 0 to 511, never falling along the last dimension, each value on 1 to 64 neighbouring positions
- image_flags: int32 [8192], P('section'), may hold values 0 or 1
- cache_length: int32 [32], P('section'), may hold values from 1024 to 2048, as said below
- query_weight: bfloat16 [65536, 8192], P('section', 'head'), may hold values from -0.09375 to 0.09375
- kv_weight: bfloat16 [65536, 1024], P('section', 'head'), may hold values from -0.09375 to 0.09375
- norm_gain: bfloat16 [65536], P('section'), may hold values from 0.5 to 1.5
- layer_input: bfloat16 [8192, 4096], P(('section', 'head')), may hold values from -6 to 6
- residual_grad: bfloat16 [8192, 4096], P(('section', 'head')), may hold values from -3 to 3
Outputs:
- input_grad: bfloat16 [8192, 4096], P(('section', 'head'))
The draws below stay inside these ranges and needn't reach their ends.
Inputs may be any that keep to these rules, and one draw needn't show every extreme that they name: `cache_length`: the two section indices 2 k and 2 k + 1 hold the same count; some section holds 2048.
All inputs are finite; a program needn't handle non-finite values. No bound on the sum of `image_flags` on one device may be relied on, other than what follows from the above.
Results may differ from the reference program's by a relative error of at most 0.0047.
Values may be sent and summed in bfloat16 or wider, within the bound.
A program may use at most 64 MiB of HBM per device.

```python
import math
import jax
import jax.numpy as jnp
import numpy as np
from jax import lax

D = 4096
HQ = 64
KVH = 4
HD = 128
SL = 256
CTX = 2048
TOKENS = 8192
KEY_ROWS = 40960
WEIGHT_ROWS = 65536
N_SECTION = 32


def draw_key_cache(key, part):
    values_drawn = jnp.clip(jax.random.normal(jax.random.fold_in(key, 11), (KEY_ROWS, KVH * HD), jnp.float32), -4.0, 4.0)
    return values_drawn.astype(jnp.bfloat16)


def draw_held_query(key, part):
    values_drawn = jnp.clip(jax.random.normal(jax.random.fold_in(key, 13), (TOKENS, HQ * HD), jnp.float32), -4.0, 4.0)
    return values_drawn.astype(jnp.bfloat16)


def draw_cache_length(key, part):
    sections = N_SECTION // 2
    counts = jax.random.randint(jax.random.fold_in(key, 17), (sections,), CTX // 2, CTX + 1)
    where_full = jax.random.randint(jax.random.fold_in(key, 19), (), 0, sections)
    counts = jnp.where(jnp.arange(sections) == where_full, CTX, counts)
    return jnp.repeat(counts, 2).astype(jnp.int32)


def set_ends(entries, rng, smallest, top_value):
    index_at = [jax.random.randint(jax.random.fold_in(rng, axis), (), 0, length) for axis, length in enumerate(entries.shape)]
    main_axis = entries.shape.index(max(entries.shape))
    next_to = index_at[:main_axis] + [(index_at[main_axis] + 1) % entries.shape[main_axis]] + index_at[main_axis + 1:]
    return entries.at[tuple(index_at)].set(smallest).at[tuple(next_to)].set(top_value)


def level_of(key, dims, shards, smallest, high):
    gain, own = 1.0, jax.random.fold_in(key, 6)
    for dim, blocks in shards:
        heights = jnp.exp(jax.random.uniform(jax.random.fold_in(own, dim), (blocks,), jnp.float32, smallest / len(shards), high / len(shards)))
        gain = gain * jnp.repeat(heights, dims[dim] // blocks).reshape([-1 if axis == dim else 1 for axis in range(len(dims))])
    return gain


def split_up(number_of, total, most, lean):
    weights = [(1 << 20) // math.isqrt(rank ** lean) + 1 for rank in range(2, number_of + 1)]
    surplus, holding = total - most - (number_of - 1), [1] * (number_of - 1)
    while surplus > 0:
        movable = [i for i in range(number_of - 1) if holding[i] < most]
        whole, budget = sum([weights[i] for i in movable]), surplus
        for i in movable:
            more = min(most - holding[i], max(1, budget * weights[i] // whole), surplus)
            holding[i] = holding[i] + more
            surplus = surplus - more
    return np.array([most] + holding)


def uneven_parts(key, number_of, total, reach, lean):
    if number_of == 2:
        one = jax.random.randint(key, (), max(1, total - reach), min(reach, total - 1) + 1)
        return jnp.stack([one, total - one])
    sizes = jnp.asarray(split_up(number_of, total, reach, lean), jnp.int32)
    pairs = (number_of - 1) // 2
    donor, taker = sizes[1:1 + 2 * pairs:2], sizes[2:2 + 2 * pairs:2]
    room = jnp.minimum(donor - 1, reach - taker)
    shifted = jax.random.randint(jax.random.fold_in(key, 1), (pairs,), 0, 1 << 20) % (room + 1)
    sizes = sizes.at[1:1 + 2 * pairs:2].set(donor - shifted).at[2:2 + 2 * pairs:2].set(taker + shifted)
    return sizes[jax.random.permutation(jax.random.fold_in(key, 2), number_of)]


def centred(own_key, dims, deviation, limit, cuts=(), kind=jnp.bfloat16):
    values = deviation * jax.random.normal(own_key, dims, jnp.float32)
    if cuts:
        values = values * level_of(own_key, dims, cuts, -0.22, 0.18)
    return jnp.clip(values, -limit, limit).astype(kind)


def setup_inputs(seed: int = 0) -> dict:
    key_of = jax.random.split(jax.random.key(seed), 14)
    return {
        "out_grad": centred(key_of[0], (TOKENS, HQ * HD), 1.0, 6.0, ((0, 32), (1, 16))),
        "held_query": draw_held_query(jax.random.fold_in(key_of[13], 71), 0),
        "held_output": centred(key_of[2], (TOKENS, HQ * HD), 1.0, 6.0, ((0, 32), (1, 16))),
        "key_cache": draw_key_cache(jax.random.fold_in(key_of[13], 71), 0),
        "value_cache": centred(key_of[4], (KEY_ROWS, KVH * HD), 1.0, 6.0, ((0, 512),)),
        "segment_ids": jnp.searchsorted(jnp.cumsum(uneven_parts(key_of[5], TOKENS // 16, TOKENS, 64, 0)), jnp.arange(TOKENS), side="right").astype(jnp.int32),
        "image_flags": set_ends((jax.random.randint(key_of[6], (TOKENS,), 0, 2) < 1).astype(jnp.int32), jax.random.fold_in(key_of[6], 1), 0, 1),
        "cache_length": draw_cache_length(jax.random.fold_in(key_of[13], 71), 0),
        "query_weight": centred(key_of[8], (WEIGHT_ROWS, HQ * HD), D ** -0.5, 0.09375, ((0, 32), (1, 16))),
        "kv_weight": centred(key_of[9], (WEIGHT_ROWS, 2 * KVH * HD), D ** -0.5, 0.09375, ((0, 32), (1, 16))),
        "norm_gain": jnp.clip(1.0 + 0.1 * jax.random.normal(key_of[10], (WEIGHT_ROWS,), jnp.float32), 0.5, 1.5).astype(jnp.bfloat16),
        "layer_input": centred(key_of[11], (TOKENS, D), 1.0, 6.0, ((0, 512),)),
        "residual_grad": centred(key_of[12], (TOKENS, D), 0.5, 3.0, ((0, 512),)),
    }


epsilon = 1e-06
far_negative = -1e+30

def section_backward(operands):
    queries, outputs, grads, key_section, value_section, segment, image_mask, length, q_weight, kvw_section, gain_row, inputs, residual = operands
    group_size = HQ // KVH
    factor = 1.0 / math.sqrt(HD)
    row_total = 2 * SL
    positions = jnp.arange(row_total, dtype=jnp.int32)
    cache_ok = jnp.arange(CTX, dtype=jnp.int32)[None, :] < length
    cache_ok = jnp.broadcast_to(cache_ok, (row_total, CTX))
    same_segment = segment[:, None] == segment[None, :]
    both_image = (image_mask[:, None] == 1) & (image_mask[None, :] == 1)
    slice_ok = same_segment & ((positions[None, :] <= positions[:, None]) | both_image)
    visible = jnp.concatenate([cache_ok, slice_ok], axis=1)
    query_parts = []
    key_parts = []
    value_parts = []
    for head_group in range(KVH):
        lower = head_group * group_size * HD
        upper = (head_group + 1) * group_size * HD
        query_heads = queries[:, lower:upper].reshape(row_total, group_size, HD).astype(jnp.float32)
        output_heads = outputs[:, lower:upper].reshape(row_total, group_size, HD).astype(jnp.float32)
        grad_heads = grads[:, lower:upper].reshape(row_total, group_size, HD).astype(jnp.float32)
        key_part = key_section[:, head_group * HD:(head_group + 1) * HD].astype(jnp.float32)
        value_part = value_section[:, head_group * HD:(head_group + 1) * HD].astype(jnp.float32)
        scores = jnp.einsum('agd,jd->gaj', query_heads, key_part) * factor
        scores = jnp.where(visible[None], scores, far_negative)
        row_max = lax.optimization_barrier(jnp.max(scores, axis=2, keepdims=True))
        log_total = row_max + jnp.log(lax.optimization_barrier(jnp.sum(jnp.exp(scores - row_max), axis=2, keepdims=True)))
        attn_probs = jnp.exp(scores - log_total)
        probs_rounded = attn_probs.astype(jnp.bfloat16)
        prob_grad = jnp.einsum('agd,jd->gaj', grad_heads, value_part)
        row_delta = jnp.einsum('agd,agd->ga', grad_heads, output_heads)[..., None]
        score_grad = (attn_probs * (prob_grad - row_delta) * factor).astype(jnp.bfloat16)
        query_grad = jnp.einsum('gaj,jd->agd', score_grad.astype(jnp.float32), key_part)
        query_parts.append(query_grad.astype(jnp.bfloat16).reshape(row_total, group_size * HD))
        key_parts.append(jnp.einsum('gab,agd->bd', score_grad[..., CTX:].astype(jnp.float32), query_heads))
        value_parts.append(jnp.einsum('gab,agd->bd', probs_rounded[..., CTX:].astype(jnp.float32), grad_heads))
    query_all = jnp.concatenate(query_parts, axis=1)
    kv_grad = jnp.concatenate(key_parts + value_parts, axis=1)
    kv_rounded = kv_grad.astype(jnp.bfloat16)
    normed_grad = jnp.dot(query_all, q_weight.T, preferred_element_type=jnp.float32)
    normed_grad = normed_grad + jnp.dot(kv_rounded, kvw_section.T, preferred_element_type=jnp.float32)
    values_in = inputs.astype(jnp.float32)
    inverse = lax.rsqrt(lax.optimization_barrier(jnp.mean(values_in * values_in, axis=1, keepdims=True)) + epsilon)
    weighted = gain_row.astype(jnp.float32)[None, :] * normed_grad
    result = residual.astype(jnp.float32) + inverse * weighted - values_in * inverse ** 3 * lax.optimization_barrier(jnp.mean(weighted * values_in, axis=1, keepdims=True))
    return result.astype(jnp.bfloat16)

def reference(out_grad, held_query, held_output, key_cache, value_cache, segment_ids, image_flags, cache_length, query_weight, kv_weight, norm_gain, layer_input, residual_grad):
    sections = N_SECTION // 2
    queries = held_query.reshape(sections, 2 * SL, HQ * HD)[::-1]
    outputs = held_output.reshape(sections, 2 * SL, HQ * HD)[::-1]
    grads = out_grad.reshape(sections, 2 * SL, HQ * HD)
    key_section = key_cache.reshape(sections, CTX + 2 * SL, KVH * HD)
    value_section = value_cache.reshape(sections, CTX + 2 * SL, KVH * HD)
    segment = segment_ids.reshape(sections, 2 * SL)
    image_mask = image_flags.reshape(sections, 2 * SL)
    lengths = cache_length.reshape(sections, 2)[:, 0]
    q_weight = query_weight.reshape(sections, D, HQ * HD)
    kvw_section = kv_weight.reshape(sections, D, 2 * KVH * HD)
    gain_row = norm_gain.reshape(sections, D)
    inputs = layer_input.reshape(sections, 2 * SL, D)
    residual = residual_grad.reshape(sections, 2 * SL, D)
    result = lax.map(section_backward, (queries, outputs, grads, key_section, value_section, segment, image_mask, lengths, q_weight, kvw_section, gain_row, inputs, residual))
    return result.reshape(N_SECTION * SL, D)
```

```python
import math

import jax
import jax.numpy as jnp
from jax import lax
from jax.experimental import pallas as pl
from jax.experimental.pallas import tpu as pltpu
from jax.sharding import PartitionSpec as P

MESH = pl.DeviceIdType.MESH
BF16, F32 = jnp.bfloat16, jnp.float32

KVH = 4
HD = 128
SL = 256
CTX = 2048
D = 4096
LOCAL = 4
HEADS = 16
RING = 8
GROUP = HEADS // KVH
OWN = (CTX + 2 * SL) // 2 // HEADS
HALF = (CTX + 2 * SL) // 2
WINDOW = 384
CHUNK = 512
BLOCK = 512
BLOCKS = D // BLOCK

epsilon = 1e-06
far_negative = -1e30
factor = 1.0 / math.sqrt(HD)
factor2 = factor / math.log(2.0)


def x_first(block):
    return block % 2 == 0


def dot_nt(left, right):
    return lax.dot_general(left, right, (((1,), (1,)), ((), ())), preferred_element_type=F32)


def dot_tn(left, right):
    return lax.dot_general(left, right, (((0,), (0,)), ((), ())), preferred_element_type=F32)


def kernel(
    out_grad,
    held_query,
    held_output,
    key_cache,
    value_cache,
    code_row,
    length,
    query_weight,
    kv_weight,
    gain,
    layer_input,
    residual,
    result,
    queries,
    outputs,
    grads,
    keys,
    values,
    q_rows,
    kv_rows,
    codes,
    gains,
    scores,
    bias,
    query_grad,
    kv_acc,
    kv_other,
    kv_out,
    kv_in,
    acc,
    x_out,
    x_in,
    ring_out,
    ring_in,
    normed,
    own_sem,
    mirror_send,
    mirror_recv,
    gather_send,
    gather_recv,
    pair_send,
    pair_recv,
    share_send,
    share_recv,
    ring_send,
    ring_recv,
    x_send,
    x_recv,
):
    section = lax.axis_index("section")
    head = lax.axis_index("head")
    core = section % 2
    ring_at = head // 2
    side = head % 2
    mirror = (30 - section + 2 * core, head)
    pair = (section + 1 - 2 * core, head)
    across = (section, head + 1 - 2 * side)
    along = ((section, (head + 2) % HEADS), (section, (head + HEADS - 2) % HEADS))

    barrier = pltpu.get_barrier_semaphore()
    peers = [mirror, pair] + [(section, (head + i) % HEADS) for i in range(1, HEADS)]
    for peer in peers:
        pl.semaphore_signal(barrier, inc=1, device_id=peer, device_id_type=MESH)

    def mine(i, source, target):
        return pltpu.make_async_copy(source, target, own_sem.at[i])

    def remote(source, target, send, recv, device):
        return pltpu.make_async_remote_copy(
            src_ref=source, dst_ref=target, send_sem=send, recv_sem=recv,
            device_id=device, device_id_type=MESH,
        )

    def grad_copy(n):
        return mine(n, out_grad.at[:, pl.ds(n * HD, HD)], grads.at[n])

    own_half = pl.ds(core * (D // 2), D // 2)
    own_weights = [
        mine(LOCAL, query_weight, q_rows.at[own_half]),
        mine(LOCAL + 1, kv_weight, kv_rows.at[own_half]),
    ]
    for n in range(LOCAL):
        grad_copy(n).start()
    for copy in own_weights:
        copy.start()
    codes[core] = jnp.broadcast_to(code_row[...], (8, SL))
    gains[core] = gain[...]

    pl.semaphore_wait(barrier, len(peers))

    def from_mirror(which, n):
        source, target = ((held_query, queries), (held_output, outputs))[which]
        return remote(
            source.at[:, pl.ds(n * HD, HD)], target.at[n],
            mirror_send.at[which, n], mirror_recv.at[which, n], mirror,
        )

    own_rows = pl.ds(pl.multiple_of(core * HALF + head * OWN, 16), OWN)
    cached = ((key_cache, keys), (value_cache, values))
    for which, (source, target) in enumerate(cached):
        for i in range(1, HEADS):
            to = (head + i) % HEADS
            columns = pl.ds(pl.multiple_of(to // GROUP * HD, HD), HD)
            remote(
                source.at[:, columns], target.at[own_rows],
                gather_send.at[which], gather_recv.at[which], (section, to),
            ).start()
        columns = pl.ds(pl.multiple_of(head // GROUP * HD, HD), HD)
        pltpu.make_async_copy(
            source.at[:, columns], target.at[own_rows], gather_recv.at[which]
        ).start()

    for n in range(LOCAL):
        for which in range(2):
            from_mirror(which, n).start()

    pair_copies = [
        remote(codes.at[core], codes.at[core], pair_send.at[0], pair_recv.at[0], pair),
        remote(gains.at[core], gains.at[core], pair_send.at[1], pair_recv.at[1], pair),
        remote(query_weight, q_rows.at[own_half], pair_send.at[2], pair_recv.at[2], pair),
        remote(kv_weight, kv_rows.at[own_half], pair_send.at[3], pair_recv.at[3], pair),
    ]
    for copy in pair_copies:
        copy.start()

    pair_copies[0].wait_recv()
    here = codes[core][0:1]
    at_row = lax.broadcasted_iota(jnp.int32, (SL, SL), 0)
    at_lane = lax.broadcasted_iota(jnp.int32, (SL, SL), 1)
    code_column = jnp.sum(
        jnp.where(at_row == at_lane, here.astype(F32), 0.0), axis=1, keepdims=True
    ).astype(jnp.int32)
    both = jnp.concatenate([codes[0][0:1], codes[1][0:1]], axis=1)
    code_keys = jnp.where(core == 0, both[:, :WINDOW], both[:, 2 * SL - WINDOW :])
    token = core * SL + lax.broadcasted_iota(jnp.int32, (SL, WINDOW), 0)
    key_at = core * (2 * SL - WINDOW) + lax.broadcasted_iota(jnp.int32, (SL, WINDOW), 1)
    same_segment = (code_column >> 1) == (code_keys >> 1)
    both_image = (code_column & 1) + (code_keys & 1) == 2
    seen = same_segment & ((key_at <= token) | both_image)
    bias[...] = jnp.where(seen, 0.0, far_negative)
    kv_acc[...] = jnp.zeros_like(kv_acc)

    half_rows = pl.ds(pl.multiple_of(core * HALF, 16), HALF)
    for which, (_, target) in enumerate(cached):
        half = target.at[half_rows]
        pltpu.make_async_copy(half, half, gather_recv.at[which]).wait()
        remote(half, half, pair_send.at[4 + which], pair_recv.at[4 + which], pair).start()
    for which, (_, target) in enumerate(cached):
        half = target.at[half_rows]
        remote(half, half, pair_send.at[4 + which], pair_recv.at[4 + which], pair).wait()

    window_rows = pl.ds(pl.multiple_of(CTX + core * (2 * SL - WINDOW), 16), WINDOW)
    chunks = [(pl.ds(i, CHUNK), slice(i, i + CHUNK)) for i in range(0, CTX, CHUNK)]
    chunks.append((window_rows, slice(CTX, CTX + WINDOW)))

    def tiles(array):
        return [array[:, i : i + HD] for i in range(0, array.shape[1], HD)]

    def attention(n, carry):
        from_mirror(0, n).wait()
        query = queries[n]
        most = None
        for rows, columns in chunks:
            raw = dot_nt(query, keys[rows])
            if columns.start == CTX:
                raw = raw + bias[...]
            elif columns.stop > CTX // 2:
                at = columns.start + lax.broadcasted_iota(jnp.int32, (1, CHUNK), 1)
                raw = raw + jnp.where(at < length[0], 0.0, far_negative)
            scores[:, columns] = raw
            for tile in tiles(raw):
                most = tile if most is None else jnp.maximum(most, tile)
        most = jnp.max(most, axis=1, keepdims=True)
        total = jnp.zeros((SL, HD), F32)
        for _, columns in chunks:
            weight = jnp.exp2((scores[:, columns] - most) * factor2)
            scores[:, columns] = weight
            for tile in tiles(weight):
                total = total + tile
        total = jnp.sum(total, axis=1, keepdims=True)
        inverse = 1.0 / total
        scale = factor * inverse
        from_mirror(1, n).wait()
        grad_copy(n).wait()
        grad = grads[n]
        delta = jnp.sum(grad.astype(F32) * outputs[n].astype(F32), axis=1, keepdims=True)
        gradient = jnp.zeros((SL, HD), F32)
        for rows, columns in chunks:
            weight = scores[:, columns]
            prob_grad = dot_nt(grad, values[rows])
            score_grad = (weight * scale * (prob_grad - delta)).astype(BF16)
            gradient = gradient + jnp.dot(score_grad, keys[rows], preferred_element_type=F32)
            if columns.start == CTX:
                probs = (weight * inverse).astype(BF16)
                kv_acc[:, :HD] += dot_tn(score_grad, query)
                kv_acc[:, HD:] += dot_tn(probs, grad)
        query_grad[:, pl.ds(pl.multiple_of(n * HD, HD), HD)] = gradient.astype(BF16)
        return carry

    lax.fori_loop(0, LOCAL, attention, 0)

    other_rows = pl.ds(pl.multiple_of((1 - core) * SL, 16), WINDOW - SL)
    kv_pair = remote(kv_acc.at[other_rows], kv_other, pair_send.at[6], pair_recv.at[6], pair)
    kv_pair.start()

    for copy in own_weights:
        copy.wait()
    for copy in pair_copies[1:]:
        copy.wait_recv()

    def project(block):
        columns = slice(block * BLOCK, (block + 1) * BLOCK)
        acc[:, columns] = dot_nt(query_grad[...], q_rows[columns])

    project(0)
    kv_pair.wait_recv()
    kv_acc[WINDOW - SL : SL] += kv_other[...]
    summed = kv_acc[pl.ds(pl.multiple_of(core * (WINDOW - SL), 16), SL)]
    low = lax.broadcasted_iota(jnp.int32, (HD, HD), 1) < HD // 2
    group = head // GROUP
    place = head % GROUP
    for i in range(4):
        columns = slice(i // 2 * HD, (i // 2 + 1) * HD)
        top, bottom = summed[: SL // 2, columns], summed[SL // 2 :, columns]
        if i % 2 == 0:
            packed = jnp.where(low, top, pltpu.roll(bottom, HD // 2, 1))
        else:
            packed = jnp.where(low, pltpu.roll(top, HD // 2, 1), bottom)
        kv_out[i] = packed.astype(BF16)

    def share(i):
        to = i // 2 * (HEADS // 2) + 2 * group + i % 2
        copy = remote(
            kv_out.at[i], kv_in.at[place], share_send.at[i], share_recv.at[place], (section, to)
        )
        local = pltpu.make_async_copy(kv_out.at[i], kv_in.at[place], share_recv.at[place])
        return to, copy, local

    for i in range(4):
        to, copy, local = share(i)
        pl.when(to != head)(copy.start)
        pl.when(to == head)(local.start)
    for block in range(1, BLOCKS):
        project(block)
    for i in range(4):
        pltpu.make_async_copy(kv_out.at[i], kv_in.at[i], share_recv.at[i]).wait()
    kv_sum = kv_in[0].astype(F32) + kv_in[1].astype(F32) + kv_in[2].astype(F32) + kv_in[3].astype(F32)
    kv_part = jnp.concatenate(
        [kv_sum[:, : HD // 2], pltpu.roll(kv_sum, HD // 2, 1)[:, : HD // 2]], axis=0
    ).astype(BF16)

    def columns_of(block):
        return slice(block * BLOCK, (block + 1) * BLOCK)

    def own_part(block, at):
        if x_first(block):
            rows = pl.ds(pl.multiple_of(at * 32 + side * 16, 16), 16)
        else:
            rows = pl.ds(pl.multiple_of(at * 32, 32), 32)
        return acc[rows, columns_of(block)]

    def ring_copy(way, step, block):
        height = 16 if x_first(block) else 32
        start = block * BLOCK
        if step == 1:
            columns = pl.ds(start + way * (BLOCK // 2), BLOCK // 2)
        else:
            columns = pl.ds(start, BLOCK)
        return remote(
            ring_out.at[way, step - 1, pl.ds(0, height), columns],
            ring_in.at[way, step - 1, pl.ds(0, height), columns],
            ring_send.at[way, step - 1, block], ring_recv.at[way, step - 1, block], along[way],
        )

    def ring_step(step, block):
        height = 16 if x_first(block) else 32
        columns = columns_of(block)
        for way in range(2):
            distance = 5 - step
            at = (ring_at + (distance if way == 0 else RING - distance)) % RING
            part = own_part(block, at)
            near = slice(columns.start + way * (BLOCK // 2), columns.start + (way + 1) * (BLOCK // 2))
            if step == 1:
                half = part[:, way * (BLOCK // 2) : (way + 1) * (BLOCK // 2)]
                ring_out[way, 0, :height, near] = half.astype(BF16)
            else:
                ring_copy(way, step - 1, block).wait_recv()
                if step == 2:
                    came = ring_in[way, 0, :height, near].astype(F32)
                    halves = [part[:, : BLOCK // 2], part[:, BLOCK // 2 :]]
                    halves[way] = halves[way] + came
                    part = jnp.concatenate(halves, axis=1)
                else:
                    part = part + ring_in[way, step - 2, :height, columns].astype(F32)
                ring_out[way, step - 1, :height, columns] = part.astype(BF16)
            ring_copy(way, step, block).start()

    def x_copy(block):
        height = 128 if x_first(block) else 16
        place = pl.ds(0, height), pl.ds(block * BLOCK, BLOCK)
        return remote(x_out.at[place], x_in.at[place], x_send.at[block], x_recv.at[block], across)

    def begin(block):
        columns = columns_of(block)
        acc[:, columns] += dot_nt(kv_part, kv_rows[columns])
        if x_first(block):
            for i in range(RING):
                rows = pl.ds(pl.multiple_of(i * 32 + (1 - side) * 16, 16), 16)
                x_out[i * 16 : (i + 1) * 16, columns] = acc[rows, columns].astype(BF16)
            x_copy(block).start()
        else:
            ring_step(1, block)

    def after_x(block):
        columns = columns_of(block)
        x_copy(block).wait_recv()
        for i in range(RING):
            rows = pl.ds(pl.multiple_of(i * 32 + side * 16, 16), 16)
            acc[rows, columns] += x_in[i * 16 : (i + 1) * 16, columns].astype(F32)
        ring_step(1, block)

    def arrived(block):
        height = 16 if x_first(block) else 32
        columns = columns_of(block)
        part = own_part(block, ring_at)
        for way in range(2):
            ring_copy(way, 4, block).wait_recv()
            part = part + ring_in[way, 3, :height, columns].astype(F32)
        return part

    def end_ring(block):
        columns = columns_of(block)
        part = arrived(block)
        if x_first(block):
            normed[:, columns] = part
        else:
            normed[:, columns] = jnp.where(side == 0, part[:16], part[16:])
            x_out[:16, columns] = jnp.where(side == 0, part[16:], part[:16]).astype(BF16)
            x_copy(block).start()

    def end_x(block):
        columns = columns_of(block)
        x_copy(block).wait_recv()
        normed[:, columns] += x_in[:16, columns].astype(F32)

    def actions(block):
        ring = [lambda s=s: ring_step(s, block) for s in range(2, 5)]
        if x_first(block):
            return [lambda: begin(block), lambda: after_x(block), *ring, lambda: end_ring(block)]
        return [lambda: begin(block), *ring, lambda: end_ring(block), lambda: end_x(block)]

    plans = [actions(block) for block in range(BLOCKS)]
    for turn in range(BLOCKS + 5):
        for stage in range(6):
            if 0 <= turn - stage < BLOCKS:
                plans[turn - stage][stage]()

    values_in = layer_input[...].astype(F32)
    inverse = lax.rsqrt(jnp.sum(values_in * values_in, axis=1, keepdims=True) / D + epsilon)
    correlation = jnp.zeros((16, HD), F32)
    for t in range(D // HD):
        columns = slice(t * HD, (t + 1) * HD)
        row = gains[t // 16].astype(F32)[t % 16 : t % 16 + 1]
        weighted = row * normed[:, columns]
        normed[:, columns] = weighted
        correlation = correlation + weighted * values_in[:, columns]
    mean = jnp.sum(correlation, axis=1, keepdims=True) / D
    result[...] = (
        residual[...].astype(F32)
        + inverse * normed[...]
        - values_in * (inverse * inverse * inverse * mean)
    ).astype(BF16)

    for which, (_, target) in enumerate(cached):
        sent = target.at[pl.ds(0, (HEADS - 1) * OWN)]
        pltpu.make_async_copy(sent, sent, gather_send.at[which]).wait()
    for copy in [*pair_copies, kv_pair]:
        copy.wait_send()
    for i in range(4):
        to, copy, _ = share(i)
        pl.when(to != head)(copy.wait_send)
    for block in range(BLOCKS):
        x_copy(block).wait_send()
        for way in range(2):
            for step in range(1, 5):
                ring_copy(way, step, block).wait_send()


def body(
    out_grad,
    held_query,
    held_output,
    key_cache,
    value_cache,
    segment_ids,
    image_flags,
    cache_length,
    query_weight,
    kv_weight,
    norm_gain,
    layer_input,
    residual_grad,
):
    code_row = (segment_ids * 2 + image_flags).reshape(1, SL)
    gain = norm_gain.reshape(16, HD)
    hbm = pl.BlockSpec(memory_space=pl.ANY)
    vmem = pl.BlockSpec(memory_space=pltpu.VMEM)
    smem = pl.BlockSpec(memory_space=pltpu.SMEM)
    dma = pltpu.SemaphoreType.DMA
    return pl.pallas_call(
        kernel,
        out_shape=jax.ShapeDtypeStruct(layer_input.shape, BF16),
        in_specs=[hbm, hbm, hbm, hbm, hbm, vmem, smem, hbm, hbm, vmem, vmem, vmem],
        out_specs=vmem,
        scratch_shapes=[
            pltpu.VMEM((LOCAL, SL, HD), BF16),
            pltpu.VMEM((LOCAL, SL, HD), BF16),
            pltpu.VMEM((LOCAL, SL, HD), BF16),
            pltpu.VMEM((CTX + 2 * SL, HD), BF16),
            pltpu.VMEM((CTX + 2 * SL, HD), BF16),
            pltpu.VMEM((D, LOCAL * HD), BF16),
            pltpu.VMEM((D, HD // 2), BF16),
            pltpu.VMEM((2, 8, SL), jnp.int32),
            pltpu.VMEM((2, 16, HD), BF16),
            pltpu.VMEM((SL, CTX + WINDOW), F32),
            pltpu.VMEM((SL, WINDOW), F32),
            pltpu.VMEM((SL, LOCAL * HD), BF16),
            pltpu.VMEM((WINDOW, 2 * HD), F32),
            pltpu.VMEM((WINDOW - SL, 2 * HD), F32),
            pltpu.VMEM((4, HD, HD), BF16),
            pltpu.VMEM((4, HD, HD), BF16),
            pltpu.VMEM((SL, D), F32),
            pltpu.VMEM((128, D), BF16),
            pltpu.VMEM((128, D), BF16),
            pltpu.VMEM((2, 4, 32, D), BF16),
            pltpu.VMEM((2, 4, 32, D), BF16),
            pltpu.VMEM((16, D), F32),
            dma((LOCAL + 2,)),
            dma((2, LOCAL)),
            dma((2, LOCAL)),
            dma((2,)),
            dma((2,)),
            dma((7,)),
            dma((7,)),
            dma((4,)),
            dma((4,)),
            dma((2, 4, BLOCKS)),
            dma((2, 4, BLOCKS)),
            dma((BLOCKS,)),
            dma((BLOCKS,)),
        ],
        compiler_params=pltpu.CompilerParams(
            collective_id=0, has_side_effects=True, vmem_limit_bytes=48 * 1024 * 1024
        ),
    )(
        out_grad,
        held_query,
        held_output,
        key_cache,
        value_cache,
        code_row,
        cache_length,
        query_weight,
        kv_weight,
        gain,
        layer_input,
        residual_grad,
    )


def solution(mesh):
    both = ("section", "head")
    in_specs = (
        P(*both),
        P(*both),
        P(*both),
        P(both, None),
        P(both, None),
        P("section"),
        P("section"),
        P("section"),
        P(*both),
        P(*both),
        P("section"),
        P(both, None),
        P(both, None),
    )
    return jax.shard_map(
        body, mesh=mesh, in_specs=in_specs, out_specs=P(both, None), check_vma=False
    )
```

```python
import math

import jax
import jax.numpy as jnp
from jax import lax
from jax.experimental import pallas as pl
from jax.experimental.pallas import tpu as pltpu
from jax.sharding import PartitionSpec as P

MESH = pl.DeviceIdType.MESH
BF16, F32 = jnp.bfloat16, jnp.float32

KVH = 4
HD = 128
SL = 256
CTX = 2048
D = 4096
LOCAL = 4
HEADS = 16
RING = 8
GROUP = HEADS // KVH
OWN = (CTX + 2 * SL) // 2 // HEADS
HALF = (CTX + 2 * SL) // 2
REACH = 64
WINDOW = 384
CHUNK = 512
BLOCK = 512
BLOCKS = D // BLOCK

epsilon = 1e-06
far_negative = -1e30
factor = 1.0 / math.sqrt(HD)
factor2 = factor / math.log(2.0)


TURNS = tuple([0, 1, 2, 3, 4, 5, 6, 7, 1, 2, 3, 5, 6, 7, 0, 1, 2, 3, 5, 4, 6, 7, 0, 1, 2, 3, 5, 4, 6, 7, 0, 1, 2, 3, 5, 1, 4, 2, 6, 3, 7, 0, 5, 4, 6, 7, 0, 4])


def x_first(block):
    return block in (0, 4)


def dot_nt(left, right):
    return lax.dot_general(left, right, (((1,), (1,)), ((), ())), preferred_element_type=F32)


def dot_tn(left, right):
    return lax.dot_general(left, right, (((0,), (0,)), ((), ())), preferred_element_type=F32)


def kernel(
    out_grad,
    held_query,
    held_output,
    key_cache,
    value_cache,
    segments,
    flags,
    length,
    query_weight,
    kv_weight,
    gain,
    layer_input,
    residual,
    result,
    queries,
    outputs,
    grads,
    keys,
    values,
    q_rows,
    kv_rows,
    codes,
    gains,
    scores,
    bias,
    query_grad,
    kv_acc,
    kv_out,
    kv_in,
    reach_out,
    reach_in,
    segments_here,
    flags_here,
    input_here,
    residual_here,
    acc,
    x_out,
    x_in,
    ring_out,
    ring_in,
    normed,
    own_sem,
    mirror_send,
    mirror_recv,
    gather_send,
    gather_recv,
    pair_send,
    pair_recv,
    home_send,
    home_recv,
    share_send,
    share_recv,
    ring_send,
    ring_recv,
    x_send,
    x_recv,
):
    section = lax.axis_index("section")
    head = lax.axis_index("head")
    core = section % 2
    ring_at = head // 2
    side = head % 2
    mirror = (30 - section + 2 * core, head)
    pair = (section + 1 - 2 * core, head)
    across = (section, head + 1 - 2 * side)
    along = ((section, (head + 2) % HEADS), (section, (head + HEADS - 2) % HEADS))

    barrier = pltpu.get_barrier_semaphore()
    group_start = head // GROUP * GROUP
    peers = [mirror] + [(section, (head + i) % HEADS) for i in range(1, HEADS)]
    peers += [(pair[0], group_start + (head + i) % GROUP) for i in range(GROUP)]
    for peer in peers:
        pl.semaphore_signal(barrier, inc=1, device_id=peer, device_id_type=MESH)

    def mine(i, source, target):
        return pltpu.make_async_copy(source, target, own_sem.at[i])

    def remote(source, target, send, recv, device):
        return pltpu.make_async_remote_copy(
            src_ref=source, dst_ref=target, send_sem=send, recv_sem=recv,
            device_id=device, device_id_type=MESH,
        )

    def grad_copy(n):
        return mine(n, out_grad.at[:, pl.ds(n * HD, HD)], grads.at[n])

    own_half = pl.ds(pl.multiple_of(core * (D // 2), D // 2), D // 2)
    own_weight = mine(LOCAL, query_weight, q_rows.at[own_half])
    for n in range(LOCAL):
        grad_copy(n).start()
    own_weight.start()
    small = [
        mine(LOCAL + 1, segments, segments_here),
        mine(LOCAL + 2, flags, flags_here),
        mine(LOCAL + 3, gain, gains.at[core]),
        mine(LOCAL + 4, layer_input, input_here),
        mine(LOCAL + 5, residual, residual_here),
    ]
    for copy in small:
        copy.start()
    pl.semaphore_wait(barrier, len(peers))

    def from_mirror(which, n):
        source, target = ((held_query, queries), (held_output, outputs))[which]
        return remote(
            source.at[:, pl.ds(n * HD, HD)], target.at[n],
            mirror_send.at[which, n], mirror_recv.at[which, n], mirror,
        )

    own_rows = pl.ds(pl.multiple_of(core * HALF + head * OWN, 16), OWN)
    cached = ((key_cache, keys), (value_cache, values))
    for which, (source, target) in enumerate(cached):
        for i in range(1, HEADS):
            to = (head + i) % HEADS
            columns = pl.ds(pl.multiple_of(to // GROUP * HD, HD), HD)
            remote(
                source.at[:, columns], target.at[own_rows],
                gather_send.at[which], gather_recv.at[which], (section, to),
            ).start()
        columns = pl.ds(pl.multiple_of(head // GROUP * HD, HD), HD)
        pltpu.make_async_copy(
            source.at[:, columns], target.at[own_rows], gather_recv.at[which]
        ).start()

    for n in range(LOCAL):
        for which in range(2):
            from_mirror(which, n).start()

    quarter = head // (HEADS // 2) * 2 + head % 2
    kv_home = head % (HEADS // 2) // 2 * GROUP + quarter
    kv_half = kv_rows.at[:, own_half]
    kv_away = remote(kv_weight, kv_half, home_send, home_recv, (section, kv_home))
    kv_here = pltpu.make_async_copy(kv_weight, kv_half, home_recv)
    kv_arrival = pltpu.make_async_copy(kv_half, kv_half, home_recv)
    kv_forward = remote(kv_half, kv_half, pair_send.at[3], pair_recv.at[3], pair)
    pl.when(kv_home != head)(kv_away.start)
    pl.when(kv_home == head)(kv_here.start)

    small[0].wait()
    small[1].wait()
    codes[core] = jnp.broadcast_to(segments_here[...] * 2 + flags_here[...], (8, SL))
    small[2].wait()
    pair_copies = [
        remote(codes.at[core], codes.at[core], pair_send.at[0], pair_recv.at[0], pair),
        remote(gains.at[core], gains.at[core], pair_send.at[1], pair_recv.at[1], pair),
        remote(query_weight, q_rows.at[own_half], pair_send.at[2], pair_recv.at[2], pair),
    ]
    for copy in pair_copies:
        copy.start()

    pair_copies[0].wait_recv()
    here = codes[core][0:1]
    at_row = lax.broadcasted_iota(jnp.int32, (SL, SL), 0)
    at_lane = lax.broadcasted_iota(jnp.int32, (SL, SL), 1)
    code_column = jnp.sum(
        jnp.where(at_row == at_lane, here.astype(F32), 0.0), axis=1, keepdims=True
    ).astype(jnp.int32)
    both = jnp.concatenate([codes[0][0:1], codes[1][0:1]], axis=1)
    code_keys = jnp.where(core == 0, both[:, :WINDOW], both[:, 2 * SL - WINDOW :])
    token = core * SL + lax.broadcasted_iota(jnp.int32, (SL, WINDOW), 0)
    key_at = core * (2 * SL - WINDOW) + lax.broadcasted_iota(jnp.int32, (SL, WINDOW), 1)
    same_segment = (code_column >> 1) == (code_keys >> 1)
    both_image = (code_column & 1) + (code_keys & 1) == 2
    seen = same_segment & ((key_at <= token) | both_image)
    bias[...] = jnp.where(seen, 0.0, far_negative)
    kv_acc[...] = jnp.zeros_like(kv_acc)

    half_rows = pl.ds(pl.multiple_of(core * HALF, 16), HALF)
    for which, (_, target) in enumerate(cached):
        half = target.at[half_rows]
        pltpu.make_async_copy(half, half, gather_recv.at[which]).wait()
        remote(half, half, pair_send.at[4 + which], pair_recv.at[4 + which], pair).start()
    for which, (_, target) in enumerate(cached):
        half = target.at[half_rows]
        remote(half, half, pair_send.at[4 + which], pair_recv.at[4 + which], pair).wait()

    window_rows = pl.ds(pl.multiple_of(CTX + core * (2 * SL - WINDOW), 16), WINDOW)
    chunks = [(pl.ds(i, CHUNK), slice(i, i + CHUNK)) for i in range(0, CTX, CHUNK)]
    chunks.append((window_rows, slice(CTX, CTX + WINDOW)))

    def tiles(array):
        return [array[:, i : i + HD] for i in range(0, array.shape[1], HD)]

    def attention(n, carry):
        from_mirror(0, n).wait()
        query = queries[n]
        most = None
        for rows, columns in chunks:
            raw = dot_nt(query, keys[rows])
            if columns.start == CTX:
                raw = raw + bias[...]
            elif columns.stop > CTX // 2:
                at = columns.start + lax.broadcasted_iota(jnp.int32, (1, CHUNK), 1)
                raw = raw + jnp.where(at < length[0], 0.0, far_negative)
            scores[:, columns] = raw
            for tile in tiles(raw):
                most = tile if most is None else jnp.maximum(most, tile)
        most = jnp.max(most, axis=1, keepdims=True)
        total = jnp.zeros((SL, HD), F32)
        for _, columns in chunks:
            weight = jnp.exp2((scores[:, columns] - most) * factor2)
            scores[:, columns] = weight
            for tile in tiles(weight):
                total = total + tile
        total = jnp.sum(total, axis=1, keepdims=True)
        inverse = 1.0 / total
        scale = factor * inverse
        from_mirror(1, n).wait()
        grad_copy(n).wait()
        grad = grads[n]
        delta = jnp.sum(grad.astype(F32) * outputs[n].astype(F32), axis=1, keepdims=True)
        gradient = jnp.zeros((SL, HD), F32)
        for rows, columns in chunks:
            weight = scores[:, columns]
            prob_grad = dot_nt(grad, values[rows])
            score_grad = (weight * scale * (prob_grad - delta)).astype(BF16)
            gradient = gradient + jnp.dot(score_grad, keys[rows], preferred_element_type=F32)
            if columns.start == CTX:
                probs = (weight * inverse).astype(BF16)
                kv_acc[:, :HD] += dot_tn(score_grad, query)
                kv_acc[:, HD:] += dot_tn(probs, grad)
        query_grad[:, pl.ds(pl.multiple_of(n * HD, HD), HD)] = gradient.astype(BF16)
        return carry

    lax.fori_loop(0, LOCAL, attention, 0)

    kv_arrival.wait()
    kv_forward.start()
    own_weight.wait()
    for copy in pair_copies[1:]:
        copy.wait_recv()

    def project(block):
        columns = slice(block * BLOCK, (block + 1) * BLOCK)
        acc[:, columns] = dot_nt(query_grad[...], q_rows[columns])

    own_keys = kv_acc[pl.ds(pl.multiple_of(core * (WINDOW - SL), 16), SL)]
    other_keys = kv_acc[pl.ds(pl.multiple_of(SL - core * (SL - REACH), 16), REACH)]
    group = head // GROUP
    place = head % GROUP

    def both_lanes(array, upper):
        turned = pltpu.roll(array, HD // 2, 1)
        low = lax.broadcasted_iota(jnp.int32, array.shape, 1) < HD // 2
        return jnp.where(low, turned, array) if upper else jnp.where(low, array, turned)

    low = lax.broadcasted_iota(jnp.int32, (HD, HD), 1) < HD // 2
    for i in range(GROUP):
        columns = slice(i // 2 * HD, (i // 2 + 1) * HD)
        top = both_lanes(own_keys[: SL // 2, columns], i % 2)
        bottom = both_lanes(own_keys[SL // 2 :, columns], i % 2)
        kv_out[i] = jnp.where(low, top, bottom).astype(BF16)
        reach_out[i] = both_lanes(other_keys[:, columns], i % 2).astype(BF16)

    def share(i):
        to = group * GROUP + i
        copy = remote(
            kv_out.at[i], kv_in.at[place], share_send.at[0, i], share_recv.at[0, place],
            (section, to),
        )
        local = pltpu.make_async_copy(kv_out.at[i], kv_in.at[place], share_recv.at[0, place])
        reach = remote(
            reach_out.at[i], reach_in.at[place], share_send.at[1, i], share_recv.at[1, place],
            (pair[0], to),
        )
        return copy, local, reach

    for i in range(GROUP):
        copy, local, reach = share(i)
        pl.when(i != place)(copy.start)
        pl.when(i == place)(local.start)
        reach.start()
    for block in range(BLOCKS):
        project(block)
    kv_sum = jnp.zeros((HD, HD), F32)
    reach_sum = jnp.zeros((REACH, HD), F32)
    for i in range(GROUP):
        pltpu.make_async_copy(kv_out.at[i], kv_in.at[i], share_recv.at[0, i]).wait()
        kv_sum = kv_sum + kv_in[i].astype(F32)
        pltpu.make_async_copy(reach_out.at[i], reach_in.at[i], share_recv.at[1, i]).wait()
        reach_sum = reach_sum + reach_in[i].astype(F32)
    lane_half = lax.broadcasted_iota(jnp.int32, (REACH, HD), 1) // (HD // 2)
    reach_sum = jnp.where(lane_half == 1 - core, reach_sum, 0.0)
    second = core.astype(F32)
    kv_sum = kv_sum + jnp.concatenate([reach_sum * second, reach_sum * (1.0 - second)], axis=0)
    kv_part = jnp.concatenate(
        [kv_sum[:, : HD // 2], pltpu.roll(kv_sum, HD // 2, 1)[:, : HD // 2]], axis=0
    ).astype(BF16)
    kv_forward.wait_recv()

    def columns_of(block):
        return slice(block * BLOCK, (block + 1) * BLOCK)

    def own_part(block, at):
        if x_first(block):
            rows = pl.ds(pl.multiple_of(at * 32 + side * 16, 16), 16)
        else:
            rows = pl.ds(pl.multiple_of(at * 32, 32), 32)
        return acc[rows, columns_of(block)]

    def ring_copy(way, step, block):
        height = 16 if x_first(block) else 32
        start = block * BLOCK
        if step == 1:
            columns = pl.ds(start + way * (BLOCK // 2), BLOCK // 2)
        else:
            columns = pl.ds(start, BLOCK)
        return remote(
            ring_out.at[way, step - 1, pl.ds(0, height), columns],
            ring_in.at[way, step - 1, pl.ds(0, height), columns],
            ring_send.at[way, step - 1, block], ring_recv.at[way, step - 1, block], along[way],
        )

    def ring_step(step, block):
        height = 16 if x_first(block) else 32
        columns = columns_of(block)
        for way in range(2):
            distance = 5 - step
            at = (ring_at + (distance if way == 0 else RING - distance)) % RING
            part = own_part(block, at)
            near = slice(columns.start + way * (BLOCK // 2), columns.start + (way + 1) * (BLOCK // 2))
            if step == 1:
                half = part[:, way * (BLOCK // 2) : (way + 1) * (BLOCK // 2)]
                ring_out[way, 0, :height, near] = half.astype(BF16)
            else:
                ring_copy(way, step - 1, block).wait_recv()
                if step == 2:
                    came = ring_in[way, 0, :height, near].astype(F32)
                    halves = [part[:, : BLOCK // 2], part[:, BLOCK // 2 :]]
                    halves[way] = halves[way] + came
                    part = jnp.concatenate(halves, axis=1)
                else:
                    part = part + ring_in[way, step - 2, :height, columns].astype(F32)
                ring_out[way, step - 1, :height, columns] = part.astype(BF16)
            ring_copy(way, step, block).start()

    def x_copy(block):
        height = 128 if x_first(block) else 16
        place = pl.ds(0, height), pl.ds(block * BLOCK, BLOCK)
        return remote(x_out.at[place], x_in.at[place], x_send.at[block], x_recv.at[block], across)

    def begin(block):
        columns = columns_of(block)
        acc[:, columns] += jnp.dot(kv_part, kv_rows[:, columns], preferred_element_type=F32)
        if x_first(block):
            for i in range(RING):
                rows = pl.ds(pl.multiple_of(i * 32 + (1 - side) * 16, 16), 16)
                x_out[i * 16 : (i + 1) * 16, columns] = acc[rows, columns].astype(BF16)
            x_copy(block).start()
        else:
            ring_step(1, block)

    def after_x(block):
        columns = columns_of(block)
        x_copy(block).wait_recv()
        for i in range(RING):
            rows = pl.ds(pl.multiple_of(i * 32 + side * 16, 16), 16)
            acc[rows, columns] += x_in[i * 16 : (i + 1) * 16, columns].astype(F32)
        ring_step(1, block)

    def arrived(block):
        height = 16 if x_first(block) else 32
        columns = columns_of(block)
        part = own_part(block, ring_at)
        for way in range(2):
            ring_copy(way, 4, block).wait_recv()
            part = part + ring_in[way, 3, :height, columns].astype(F32)
        return part

    def end_ring(block):
        columns = columns_of(block)
        part = arrived(block)
        if x_first(block):
            normed[:, columns] = part
        else:
            normed[:, columns] = jnp.where(side == 0, part[:16], part[16:])
            x_out[:16, columns] = jnp.where(side == 0, part[16:], part[:16]).astype(BF16)
            x_copy(block).start()

    def end_x(block):
        columns = columns_of(block)
        x_copy(block).wait_recv()
        normed[:, columns] += x_in[:16, columns].astype(F32)

    def actions(block):
        ring = [lambda s=s: ring_step(s, block) for s in range(2, 5)]
        if x_first(block):
            return [lambda: begin(block), lambda: after_x(block), *ring, lambda: end_ring(block)]
        return [lambda: begin(block), *ring, lambda: end_ring(block), lambda: end_x(block)]

    plans = [actions(block) for block in range(BLOCKS)]
    for block in TURNS:
        plans[block].pop(0)()

    small[3].wait()
    small[4].wait()
    values_in = input_here[...].astype(F32)
    inverse = lax.rsqrt(jnp.sum(values_in * values_in, axis=1, keepdims=True) / D + epsilon)
    correlation = jnp.zeros((16, HD), F32)
    for t in range(D // HD):
        columns = slice(t * HD, (t + 1) * HD)
        row = gains[t // 16].astype(F32)[t % 16 : t % 16 + 1]
        weighted = row * normed[:, columns]
        normed[:, columns] = weighted
        correlation = correlation + weighted * values_in[:, columns]
    mean = jnp.sum(correlation, axis=1, keepdims=True) / D
    result[...] = (
        residual_here[...].astype(F32)
        + inverse * normed[...]
        - values_in * (inverse * inverse * inverse * mean)
    ).astype(BF16)

    for which, (_, target) in enumerate(cached):
        sent = target.at[pl.ds(0, (HEADS - 1) * OWN)]
        pltpu.make_async_copy(sent, sent, gather_send.at[which]).wait()
    for copy in [*pair_copies, kv_forward]:
        copy.wait_send()
    pl.when(kv_home != head)(kv_away.wait_send)
    for i in range(GROUP):
        copy, _, reach = share(i)
        pl.when(i != place)(copy.wait_send)
        reach.wait_send()
    for block in range(BLOCKS):
        x_copy(block).wait_send()
        for way in range(2):
            for step in range(1, 5):
                ring_copy(way, step, block).wait_send()


def body(
    out_grad,
    held_query,
    held_output,
    key_cache,
    value_cache,
    segment_ids,
    image_flags,
    cache_length,
    query_weight,
    kv_weight,
    norm_gain,
    layer_input,
    residual_grad,
):
    gain = norm_gain.reshape(16, HD)
    hbm = pl.BlockSpec(memory_space=pltpu.HBM)
    vmem = pl.BlockSpec(memory_space=pltpu.VMEM)
    smem = pl.BlockSpec(memory_space=pltpu.SMEM)
    dma = pltpu.SemaphoreType.DMA
    return pl.pallas_call(
        kernel,
        out_shape=jax.ShapeDtypeStruct(layer_input.shape, BF16),
        in_specs=[hbm] * 7 + [smem] + [hbm] * 5,
        out_specs=vmem,
        scratch_shapes=[
            pltpu.VMEM((LOCAL, SL, HD), BF16),
            pltpu.VMEM((LOCAL, SL, HD), BF16),
            pltpu.VMEM((LOCAL, SL, HD), BF16),
            pltpu.VMEM((CTX + 2 * SL, HD), BF16),
            pltpu.VMEM((CTX + 2 * SL, HD), BF16),
            pltpu.VMEM((D, LOCAL * HD), BF16),
            pltpu.VMEM((HD // 2, D), BF16),
            pltpu.VMEM((2, 8, SL), jnp.int32),
            pltpu.VMEM((2, 16, HD), BF16),
            pltpu.VMEM((SL, CTX + WINDOW), F32),
            pltpu.VMEM((SL, WINDOW), F32),
            pltpu.VMEM((SL, LOCAL * HD), BF16),
            pltpu.VMEM((WINDOW, 2 * HD), F32),
            pltpu.VMEM((GROUP, HD, HD), BF16),
            pltpu.VMEM((GROUP, HD, HD), BF16),
            pltpu.VMEM((GROUP, REACH, HD), BF16),
            pltpu.VMEM((GROUP, REACH, HD), BF16),
            pltpu.VMEM((1, SL), jnp.int32),
            pltpu.VMEM((1, SL), jnp.int32),
            pltpu.VMEM((16, D), BF16),
            pltpu.VMEM((16, D), BF16),
            pltpu.VMEM((SL, D), F32),
            pltpu.VMEM((128, D), BF16),
            pltpu.VMEM((128, D), BF16),
            pltpu.VMEM((2, 4, 32, D), BF16),
            pltpu.VMEM((2, 4, 32, D), BF16),
            pltpu.VMEM((16, D), F32),
            dma((LOCAL + 6,)),
            dma((2, LOCAL)),
            dma((2, LOCAL)),
            dma((2,)),
            dma((2,)),
            dma((6,)),
            dma((6,)),
            dma,
            dma,
            dma((2, GROUP)),
            dma((2, GROUP)),
            dma((2, 4, BLOCKS)),
            dma((2, 4, BLOCKS)),
            dma((BLOCKS,)),
            dma((BLOCKS,)),
        ],
        compiler_params=pltpu.CompilerParams(
            collective_id=0, has_side_effects=True, vmem_limit_bytes=60 * 1024 * 1024
        ),
    )(
        out_grad,
        held_query,
        held_output,
        key_cache,
        value_cache,
        segment_ids.reshape(1, SL),
        image_flags.reshape(1, SL),
        cache_length,
        query_weight,
        kv_weight.T,
        gain,
        layer_input,
        residual_grad,
    )


def solution(mesh):
    both = ("section", "head")
    in_specs = (
        P(*both),
        P(*both),
        P(*both),
        P(both, None),
        P(both, None),
        P("section"),
        P("section"),
        P("section"),
        P(*both),
        P(*both),
        P("section"),
        P(both, None),
        P(both, None),
    )
    return jax.shard_map(
        body, mesh=mesh, in_specs=in_specs, out_specs=P(both, None), check_vma=False
    )
```

```python
import math

import jax
import jax.numpy as jnp
from jax import lax
from jax.experimental import pallas as pl
from jax.experimental.pallas import tpu as pltpu
from jax.sharding import PartitionSpec as P

MESH = pl.DeviceIdType.MESH
BF16, F32 = jnp.bfloat16, jnp.float32

KVH = 4
HD = 128
SL = 256
CTX = 2048
D = 4096
LOCAL = 4
HEADS = 16
RING = 8
GROUP = HEADS // KVH
OWN = (CTX + 2 * SL) // 2 // HEADS
HALF = (CTX + 2 * SL) // 2
REACH = 64
WINDOW = 384
CHUNK = 512
BLOCK = 512
BLOCKS = D // BLOCK

epsilon = 1e-06
far_negative = -1e30
factor = 1.0 / math.sqrt(HD)
factor2 = factor / math.log(2.0)


TURNS = (0, 1, 2, 3, 4, 5, 6, 7, 1, 2, 3, 4, 5, 7, 0, 1, 2, 3, 6, 4, 5, 7, 0, 1, 2, 3, 6, 4, 5, 7, 0, 1, 2, 3, 6, 4, 1, 5, 2, 7, 3, 0, 6, 4, 5, 7, 0, 6)


def x_first(block):
    return block in (0, 6)


def dot_nt(left, right):
    return lax.dot_general(left, right, (((1,), (1,)), ((), ())), preferred_element_type=F32)


def dot_tn(left, right):
    return lax.dot_general(left, right, (((0,), (0,)), ((), ())), preferred_element_type=F32)


def kernel(
    out_grad,
    held_query,
    held_output,
    key_cache,
    value_cache,
    segments,
    flags,
    length,
    query_weight,
    kv_weight,
    gain,
    layer_input,
    residual,
    result,
    queries,
    outputs,
    grads,
    keys,
    values,
    q_rows,
    kv_rows,
    codes,
    gains,
    scores,
    bias,
    query_grad,
    kv_acc,
    kv_out,
    kv_in,
    reach_out,
    reach_in,
    segments_here,
    flags_here,
    input_here,
    residual_here,
    acc,
    x_out,
    x_in,
    ring_out,
    ring_in,
    normed,
    own_sem,
    mirror_send,
    mirror_recv,
    gather_send,
    gather_recv,
    pair_send,
    pair_recv,
    home_send,
    home_recv,
    share_send,
    share_recv,
    ring_send,
    ring_recv,
    x_send,
    x_recv,
):
    section = lax.axis_index("section")
    head = lax.axis_index("head")
    core = section % 2
    ring_at = head // 2
    side = head % 2
    mirror = (30 - section + 2 * core, head)
    pair = (section + 1 - 2 * core, head)
    across = (section, head + 1 - 2 * side)
    along = ((section, (head + 2) % HEADS), (section, (head + HEADS - 2) % HEADS))

    barrier = pltpu.get_barrier_semaphore()
    group_start = head // GROUP * GROUP
    peers = [mirror] + [(section, (head + i) % HEADS) for i in range(1, HEADS)]
    peers += [(pair[0], group_start + (head + i) % GROUP) for i in range(GROUP)]
    for peer in peers:
        pl.semaphore_signal(barrier, inc=1, device_id=peer, device_id_type=MESH)

    def mine(i, source, target):
        return pltpu.make_async_copy(source, target, own_sem.at[i])

    def remote(source, target, send, recv, device):
        return pltpu.make_async_remote_copy(
            src_ref=source, dst_ref=target, send_sem=send, recv_sem=recv,
            device_id=device, device_id_type=MESH,
        )

    def grad_copy(n):
        return mine(n, out_grad.at[:, pl.ds(n * HD, HD)], grads.at[n])

    own_half = pl.ds(pl.multiple_of(core * (D // 2), D // 2), D // 2)
    own_weight = mine(LOCAL, query_weight, q_rows.at[own_half])
    for n in range(LOCAL):
        grad_copy(n).start()
    own_weight.start()
    small = [
        mine(LOCAL + 1, segments, segments_here),
        mine(LOCAL + 2, flags, flags_here),
        mine(LOCAL + 3, gain, gains.at[core]),
        mine(LOCAL + 4, layer_input, input_here),
        mine(LOCAL + 5, residual, residual_here),
    ]
    for copy in small:
        copy.start()
    pl.semaphore_wait(barrier, len(peers))

    def from_mirror(which, n):
        source, target = ((held_query, queries), (held_output, outputs))[which]
        return remote(
            source.at[:, pl.ds(n * HD, HD)], target.at[n],
            mirror_send.at[which, n], mirror_recv.at[which, n], mirror,
        )

    for n in range(LOCAL):
        for which in range(2):
            from_mirror(which, n).start()

    own_rows = pl.ds(pl.multiple_of(core * HALF + head * OWN, 16), OWN)
    cached = ((key_cache, keys), (value_cache, values))
    for which, (source, target) in enumerate(cached):
        for i in range(1, HEADS):
            to = (head + i) % HEADS
            columns = pl.ds(pl.multiple_of(to // GROUP * HD, HD), HD)
            remote(
                source.at[:, columns], target.at[own_rows],
                gather_send.at[which], gather_recv.at[which], (section, to),
            ).start()
        columns = pl.ds(pl.multiple_of(head // GROUP * HD, HD), HD)
        pltpu.make_async_copy(
            source.at[:, columns], target.at[own_rows], gather_recv.at[which]
        ).start()


    quarter = head // (HEADS // 2) * 2 + head % 2
    kv_home = head % (HEADS // 2) // 2 * GROUP + quarter
    kv_half = kv_rows.at[:, own_half]
    kv_away = remote(kv_weight, kv_half, home_send, home_recv, (section, kv_home))
    kv_here = pltpu.make_async_copy(kv_weight, kv_half, home_recv)
    kv_arrival = pltpu.make_async_copy(kv_half, kv_half, home_recv)
    kv_forward = remote(kv_half, kv_half, pair_send.at[3], pair_recv.at[3], pair)

    small[0].wait()
    small[1].wait()
    codes[core] = jnp.broadcast_to(segments_here[...] * 2 + flags_here[...], (8, SL))
    small[2].wait()
    pair_copies = [
        remote(codes.at[core], codes.at[core], pair_send.at[0], pair_recv.at[0], pair),
        remote(gains.at[core], gains.at[core], pair_send.at[1], pair_recv.at[1], pair),
        remote(query_weight, q_rows.at[own_half], pair_send.at[2], pair_recv.at[2], pair),
    ]
    for copy in pair_copies:
        copy.start()

    pair_copies[0].wait_recv()
    here = codes[core][0:1]
    at_row = lax.broadcasted_iota(jnp.int32, (SL, SL), 0)
    at_lane = lax.broadcasted_iota(jnp.int32, (SL, SL), 1)
    code_column = jnp.sum(
        jnp.where(at_row == at_lane, here.astype(F32), 0.0), axis=1, keepdims=True
    ).astype(jnp.int32)
    both = jnp.concatenate([codes[0][0:1], codes[1][0:1]], axis=1)
    code_keys = jnp.where(core == 0, both[:, :WINDOW], both[:, 2 * SL - WINDOW :])
    token = core * SL + lax.broadcasted_iota(jnp.int32, (SL, WINDOW), 0)
    key_at = core * (2 * SL - WINDOW) + lax.broadcasted_iota(jnp.int32, (SL, WINDOW), 1)
    same_segment = (code_column >> 1) == (code_keys >> 1)
    both_image = (code_column & 1) + (code_keys & 1) == 2
    seen = same_segment & ((key_at <= token) | both_image)
    bias[...] = jnp.where(seen, 0.0, far_negative)
    kv_acc[...] = jnp.zeros_like(kv_acc)

    half_rows = pl.ds(pl.multiple_of(core * HALF, 16), HALF)
    for which, (_, target) in enumerate(cached):
        half = target.at[half_rows]
        pltpu.make_async_copy(half, half, gather_recv.at[which]).wait()
        remote(half, half, pair_send.at[4 + which], pair_recv.at[4 + which], pair).start()
    pl.when(kv_home != head)(kv_away.start)
    pl.when(kv_home == head)(kv_here.start)
    for which, (_, target) in enumerate(cached):
        half = target.at[half_rows]
        remote(half, half, pair_send.at[4 + which], pair_recv.at[4 + which], pair).wait()

    window_rows = pl.ds(pl.multiple_of(CTX + core * (2 * SL - WINDOW), 16), WINDOW)
    chunks = [(pl.ds(i, CHUNK), slice(i, i + CHUNK)) for i in range(0, CTX, CHUNK)]
    chunks.append((window_rows, slice(CTX, CTX + WINDOW)))

    def tiles(array):
        return [array[:, i : i + HD] for i in range(0, array.shape[1], HD)]

    def attention(n, carry):
        from_mirror(0, n).wait()
        query = queries[n]
        most = None
        for rows, columns in chunks:
            raw = dot_nt(query, keys[rows])
            if columns.start == CTX:
                raw = raw + bias[...]
            elif columns.stop > CTX // 2:
                at = columns.start + lax.broadcasted_iota(jnp.int32, (1, CHUNK), 1)
                raw = raw + jnp.where(at < length[0], 0.0, far_negative)
            scores[:, columns] = raw
            for tile in tiles(raw):
                most = tile if most is None else jnp.maximum(most, tile)
        most = jnp.max(most, axis=1, keepdims=True)
        total = jnp.zeros((SL, HD), F32)
        for _, columns in chunks:
            weight = jnp.exp2((scores[:, columns] - most) * factor2)
            scores[:, columns] = weight
            for tile in tiles(weight):
                total = total + tile
        total = jnp.sum(total, axis=1, keepdims=True)
        inverse = 1.0 / total
        scale = factor * inverse
        from_mirror(1, n).wait()
        grad_copy(n).wait()
        grad = grads[n]
        delta = jnp.sum(grad.astype(F32) * outputs[n].astype(F32), axis=1, keepdims=True)
        gradient = jnp.zeros((SL, HD), F32)
        for rows, columns in chunks:
            weight = scores[:, columns]
            prob_grad = dot_nt(grad, values[rows])
            score_grad = (weight * scale * (prob_grad - delta)).astype(BF16)
            gradient = gradient + jnp.dot(score_grad, keys[rows], preferred_element_type=F32)
            if columns.start == CTX:
                probs = (weight * inverse).astype(BF16)
                kv_acc[:, :HD] += dot_tn(score_grad, query)
                kv_acc[:, HD:] += dot_tn(probs, grad)
        query_grad[:, pl.ds(pl.multiple_of(n * HD, HD), HD)] = gradient.astype(BF16)
        return carry

    lax.fori_loop(0, LOCAL, attention, 0)

    kv_arrival.wait()
    kv_forward.start()
    own_weight.wait()
    for copy in pair_copies[1:]:
        copy.wait_recv()

    def project(block):
        columns = slice(block * BLOCK, (block + 1) * BLOCK)
        acc[:, columns] = dot_nt(query_grad[...], q_rows[columns])

    own_keys = kv_acc[pl.ds(pl.multiple_of(core * (WINDOW - SL), 16), SL)]
    other_keys = kv_acc[pl.ds(pl.multiple_of(SL - core * (SL - REACH), 16), REACH)]
    group = head // GROUP
    place = head % GROUP

    def both_lanes(array, upper):
        turned = pltpu.roll(array, HD // 2, 1)
        low = lax.broadcasted_iota(jnp.int32, array.shape, 1) < HD // 2
        return jnp.where(low, turned, array) if upper else jnp.where(low, array, turned)

    low = lax.broadcasted_iota(jnp.int32, (HD, HD), 1) < HD // 2
    for i in range(GROUP):
        columns = slice(i // 2 * HD, (i // 2 + 1) * HD)
        top = both_lanes(own_keys[: SL // 2, columns], i % 2)
        bottom = both_lanes(own_keys[SL // 2 :, columns], i % 2)
        kv_out[i] = jnp.where(low, top, bottom).astype(BF16)
        reach_out[i] = both_lanes(other_keys[:, columns], i % 2).astype(BF16)

    def share(i):
        to = group * GROUP + i
        copy = remote(
            kv_out.at[i], kv_in.at[place], share_send.at[0, i], share_recv.at[0, place],
            (section, to),
        )
        local = pltpu.make_async_copy(kv_out.at[i], kv_in.at[place], share_recv.at[0, place])
        reach = remote(
            reach_out.at[i], reach_in.at[place], share_send.at[1, i], share_recv.at[1, place],
            (pair[0], to),
        )
        return copy, local, reach

    for i in range(GROUP):
        copy, local, reach = share(i)
        pl.when(i != place)(copy.start)
        pl.when(i == place)(local.start)
        reach.start()
    for block in range(BLOCKS):
        project(block)
    kv_sum = jnp.zeros((HD, HD), F32)
    reach_sum = jnp.zeros((REACH, HD), F32)
    for i in range(GROUP):
        pltpu.make_async_copy(kv_out.at[i], kv_in.at[i], share_recv.at[0, i]).wait()
        kv_sum = kv_sum + kv_in[i].astype(F32)
        pltpu.make_async_copy(reach_out.at[i], reach_in.at[i], share_recv.at[1, i]).wait()
        reach_sum = reach_sum + reach_in[i].astype(F32)
    lane_half = lax.broadcasted_iota(jnp.int32, (REACH, HD), 1) // (HD // 2)
    reach_sum = jnp.where(lane_half == 1 - core, reach_sum, 0.0)
    second = core.astype(F32)
    kv_sum = kv_sum + jnp.concatenate([reach_sum * second, reach_sum * (1.0 - second)], axis=0)
    kv_part = jnp.concatenate(
        [kv_sum[:, : HD // 2], pltpu.roll(kv_sum, HD // 2, 1)[:, : HD // 2]], axis=0
    ).astype(BF16)
    kv_forward.wait_recv()

    def columns_of(block):
        return slice(block * BLOCK, (block + 1) * BLOCK)

    def own_part(block, at):
        if x_first(block):
            rows = pl.ds(pl.multiple_of(at * 32 + side * 16, 16), 16)
        else:
            rows = pl.ds(pl.multiple_of(at * 32, 32), 32)
        return acc[rows, columns_of(block)]

    def ring_copy(way, step, block):
        height = 16 if x_first(block) else 32
        start = block * BLOCK
        if step == 1:
            columns = pl.ds(start + way * (BLOCK // 2), BLOCK // 2)
        else:
            columns = pl.ds(start, BLOCK)
        return remote(
            ring_out.at[way, step - 1, pl.ds(0, height), columns],
            ring_in.at[way, step - 1, pl.ds(0, height), columns],
            ring_send.at[way, step - 1, block], ring_recv.at[way, step - 1, block], along[way],
        )

    def ring_step(step, block):
        height = 16 if x_first(block) else 32
        columns = columns_of(block)
        for way in range(2):
            distance = 5 - step
            at = (ring_at + (distance if way == 0 else RING - distance)) % RING
            part = own_part(block, at)
            near = slice(columns.start + way * (BLOCK // 2), columns.start + (way + 1) * (BLOCK // 2))
            if step == 1:
                half = part[:, way * (BLOCK // 2) : (way + 1) * (BLOCK // 2)]
                ring_out[way, 0, :height, near] = half.astype(BF16)
            else:
                ring_copy(way, step - 1, block).wait_recv()
                if step == 2:
                    came = ring_in[way, 0, :height, near].astype(F32)
                    halves = [part[:, : BLOCK // 2], part[:, BLOCK // 2 :]]
                    halves[way] = halves[way] + came
                    part = jnp.concatenate(halves, axis=1)
                else:
                    part = part + ring_in[way, step - 2, :height, columns].astype(F32)
                ring_out[way, step - 1, :height, columns] = part.astype(BF16)
            ring_copy(way, step, block).start()

    def x_copy(block):
        height = 128 if x_first(block) else 16
        place = pl.ds(0, height), pl.ds(block * BLOCK, BLOCK)
        return remote(x_out.at[place], x_in.at[place], x_send.at[block], x_recv.at[block], across)

    def begin(block):
        columns = columns_of(block)
        acc[:, columns] += jnp.dot(kv_part, kv_rows[:, columns], preferred_element_type=F32)
        if x_first(block):
            for i in range(RING):
                rows = pl.ds(pl.multiple_of(i * 32 + (1 - side) * 16, 16), 16)
                x_out[i * 16 : (i + 1) * 16, columns] = acc[rows, columns].astype(BF16)
            x_copy(block).start()
        else:
            ring_step(1, block)

    def after_x(block):
        columns = columns_of(block)
        x_copy(block).wait_recv()
        for i in range(RING):
            rows = pl.ds(pl.multiple_of(i * 32 + side * 16, 16), 16)
            acc[rows, columns] += x_in[i * 16 : (i + 1) * 16, columns].astype(F32)
        ring_step(1, block)

    def arrived(block):
        height = 16 if x_first(block) else 32
        columns = columns_of(block)
        part = own_part(block, ring_at)
        for way in range(2):
            ring_copy(way, 4, block).wait_recv()
            part = part + ring_in[way, 3, :height, columns].astype(F32)
        return part

    def end_ring(block):
        columns = columns_of(block)
        part = arrived(block)
        if x_first(block):
            normed[:, columns] = part
        else:
            normed[:, columns] = jnp.where(side == 0, part[:16], part[16:])
            x_out[:16, columns] = jnp.where(side == 0, part[16:], part[:16]).astype(BF16)
            x_copy(block).start()

    def end_x(block):
        columns = columns_of(block)
        x_copy(block).wait_recv()
        normed[:, columns] += x_in[:16, columns].astype(F32)

    def actions(block):
        ring = [lambda s=s: ring_step(s, block) for s in range(2, 5)]
        if x_first(block):
            return [lambda: begin(block), lambda: after_x(block), *ring, lambda: end_ring(block)]
        return [lambda: begin(block), *ring, lambda: end_ring(block), lambda: end_x(block)]

    plans = [actions(block) for block in range(BLOCKS)]
    for block in TURNS:
        plans[block].pop(0)()

    small[3].wait()
    small[4].wait()
    values_in = input_here[...].astype(F32)
    inverse = lax.rsqrt(jnp.sum(values_in * values_in, axis=1, keepdims=True) / D + epsilon)
    correlation = jnp.zeros((16, HD), F32)
    for t in range(D // HD):
        columns = slice(t * HD, (t + 1) * HD)
        row = gains[t // 16].astype(F32)[t % 16 : t % 16 + 1]
        weighted = row * normed[:, columns]
        normed[:, columns] = weighted
        correlation = correlation + weighted * values_in[:, columns]
    mean = jnp.sum(correlation, axis=1, keepdims=True) / D
    result[...] = (
        residual_here[...].astype(F32)
        + inverse * normed[...]
        - values_in * (inverse * inverse * inverse * mean)
    ).astype(BF16)

    for which, (_, target) in enumerate(cached):
        sent = target.at[pl.ds(0, (HEADS - 1) * OWN)]
        pltpu.make_async_copy(sent, sent, gather_send.at[which]).wait()
    for copy in [*pair_copies, kv_forward]:
        copy.wait_send()
    pl.when(kv_home != head)(kv_away.wait_send)
    for i in range(GROUP):
        copy, _, reach = share(i)
        pl.when(i != place)(copy.wait_send)
        reach.wait_send()
    for block in range(BLOCKS):
        x_copy(block).wait_send()
        for way in range(2):
            for step in range(1, 5):
                ring_copy(way, step, block).wait_send()


def body(
    out_grad,
    held_query,
    held_output,
    key_cache,
    value_cache,
    segment_ids,
    image_flags,
    cache_length,
    query_weight,
    kv_weight,
    norm_gain,
    layer_input,
    residual_grad,
):
    gain = norm_gain.reshape(16, HD)
    hbm = pl.BlockSpec(memory_space=pltpu.HBM)
    vmem = pl.BlockSpec(memory_space=pltpu.VMEM)
    smem = pl.BlockSpec(memory_space=pltpu.SMEM)
    dma = pltpu.SemaphoreType.DMA
    return pl.pallas_call(
        kernel,
        out_shape=jax.ShapeDtypeStruct(layer_input.shape, BF16),
        in_specs=[hbm] * 7 + [smem] + [hbm] * 5,
        out_specs=vmem,
        scratch_shapes=[
            pltpu.VMEM((LOCAL, SL, HD), BF16),
            pltpu.VMEM((LOCAL, SL, HD), BF16),
            pltpu.VMEM((LOCAL, SL, HD), BF16),
            pltpu.VMEM((CTX + 2 * SL, HD), BF16),
            pltpu.VMEM((CTX + 2 * SL, HD), BF16),
            pltpu.VMEM((D, LOCAL * HD), BF16),
            pltpu.VMEM((HD // 2, D), BF16),
            pltpu.VMEM((2, 8, SL), jnp.int32),
            pltpu.VMEM((2, 16, HD), BF16),
            pltpu.VMEM((SL, CTX + WINDOW), F32),
            pltpu.VMEM((SL, WINDOW), F32),
            pltpu.VMEM((SL, LOCAL * HD), BF16),
            pltpu.VMEM((WINDOW, 2 * HD), F32),
            pltpu.VMEM((GROUP, HD, HD), BF16),
            pltpu.VMEM((GROUP, HD, HD), BF16),
            pltpu.VMEM((GROUP, REACH, HD), BF16),
            pltpu.VMEM((GROUP, REACH, HD), BF16),
            pltpu.VMEM((1, SL), jnp.int32),
            pltpu.VMEM((1, SL), jnp.int32),
            pltpu.VMEM((16, D), BF16),
            pltpu.VMEM((16, D), BF16),
            pltpu.VMEM((SL, D), F32),
            pltpu.VMEM((128, D), BF16),
            pltpu.VMEM((128, D), BF16),
            pltpu.VMEM((2, 4, 32, D), BF16),
            pltpu.VMEM((2, 4, 32, D), BF16),
            pltpu.VMEM((16, D), F32),
            dma((LOCAL + 6,)),
            dma((2, LOCAL)),
            dma((2, LOCAL)),
            dma((2,)),
            dma((2,)),
            dma((6,)),
            dma((6,)),
            dma,
            dma,
            dma((2, GROUP)),
            dma((2, GROUP)),
            dma((2, 4, BLOCKS)),
            dma((2, 4, BLOCKS)),
            dma((BLOCKS,)),
            dma((BLOCKS,)),
        ],
        compiler_params=pltpu.CompilerParams(
            collective_id=0, has_side_effects=True, vmem_limit_bytes=60 * 1024 * 1024
        ),
    )(
        out_grad,
        held_query,
        held_output,
        key_cache,
        value_cache,
        segment_ids.reshape(1, SL),
        image_flags.reshape(1, SL),
        cache_length,
        query_weight,
        kv_weight.T,
        gain,
        layer_input,
        residual_grad,
    )


def solution(mesh):
    both = ("section", "head")
    in_specs = (
        P(*both),
        P(*both),
        P(*both),
        P(both, None),
        P(both, None),
        P("section"),
        P("section"),
        P("section"),
        P(*both),
        P(*both),
        P("section"),
        P(both, None),
        P(both, None),
    )
    return jax.shard_map(
        body, mesh=mesh, in_specs=in_specs, out_specs=P(both, None), check_vma=False
    )
```
